512 devices in a mesh: resp: 16 (over x, z_lo), pre: 16 (over y, z_hi), head: 2 (over core).
Axes of the slice: x: 4, y: 4, z: 16 (z_hi: 4, z_lo: 4; z = z_hi * 4 + z_lo), core: 2. Of those that a mesh axis runs over, the one named last changes fastest.
Arguments:
- queries: bfloat16 [16, 2048, 4096], P('resp', 'pre', 'head'), may hold values from -12 to 12
- keys: bfloat16 [16, 2048, 512], P('resp', 'pre', 'head'), may hold values from -12 to 12
- values: bfloat16 [16, 2048, 512], P('resp', 'pre', 'head'), may hold values from -6 to 6
- prefix_keys: bfloat16 [512, 512], P(('resp', 'pre'), 'head'), may hold values from -12 to 12
- prefix_values: bfloat16 [512, 512], P(('resp', 'pre'), 'head'), may hold values from -6 to 6
- grad_out: bfloat16 [16, 2048, 4096], P('resp', ('pre', 'head')), may hold values from -6 to 6
- lengths: int32 [16], P('resp'), may hold values from 256 to 2048, as said below
Outputs:
- grad_queries: bfloat16 [16, 2048, 4096], P('resp', ('pre', 'head'))
- grad_keys: bfloat16 [16, 2048, 512], P('resp', ('pre', 'head'))
- grad_values: bfloat16 [16, 2048, 512], P('resp', ('pre', 'head'))
- grad_prefix_keys: bfloat16 [512, 512], P(('resp', 'pre'), 'head')
- grad_prefix_values: bfloat16 [512, 512], P(('resp', 'pre'), 'head')
The draws below stay inside these ranges and needn't reach their ends.
Inputs may be any that keep to these rules, and one draw needn't show every extreme that they name: `lengths`: one response has all 2048 positions live in every draw.
All inputs are finite; a program needn't handle non-finite values.
Results may differ from the reference program's by a relative error of at most 0.0075.
Values may be sent and summed in bfloat16 or wider, within the bound.
A program may use at most 64 MiB of HBM per device.

```python
import math
import jax
import jax.numpy as jnp
from jax import lax

HQ = 32
HK = 4
HD = 128
RESPONSES = 16
RESP_LEN = 2048
PREFIX = 512


def draw_lengths(key, part):
    key = jax.random.fold_in(key, 11)
    first_key, second_key = jax.random.split(key)
    spread = jax.random.randint(first_key, (RESPONSES,), RESP_LEN // 8, RESP_LEN + 1, dtype=jnp.int32)
    longest = jax.random.randint(second_key, (), 0, RESPONSES, dtype=jnp.int32)
    slots = jnp.arange(RESPONSES, dtype=jnp.int32)
    return jnp.where(slots == longest, RESP_LEN, spread).astype(jnp.int32)


def steps_of(stream_key, dims, shards, least, largest):
    def one(axis_at, blocks):
        heights = jax.random.uniform(jax.random.fold_in(jax.random.fold_in(stream_key, 6), axis_at), (blocks,), jnp.float32, least / len(shards), largest / len(shards))
        return jnp.repeat(jnp.exp(heights), dims[axis_at] // blocks).reshape((-1,) + (1,) * (len(dims) - axis_at - 1))

    level = one(*shards[0])
    for cut in shards[1:]:
        level = level * one(*cut)
    return level


def gaussian(key, dims, deviation, reach, shards=(), kind=jnp.bfloat16):
    values = jax.random.normal(key, dims, jnp.float32) * deviation
    if len(shards) > 0:
        values = steps_of(key, dims, shards, -0.22, 0.18) * values
    return jnp.clip(values, min=-reach, max=reach).astype(kind)


def setup_inputs(seed: int = 0) -> dict:
    streams_of = jax.random.split(jax.random.key(seed), 8)
    return {
        "queries": gaussian(streams_of[0], (RESPONSES, RESP_LEN, HQ * HD), 2.0, 12.0, ((0, 16), (1, 16), (2, 2))),
        "keys": gaussian(streams_of[1], (RESPONSES, RESP_LEN, HK * HD), 2.0, 12.0, ((0, 16), (1, 16), (2, 2))),
        "values": gaussian(streams_of[2], (RESPONSES, RESP_LEN, HK * HD), 1.0, 6.0, ((0, 16), (1, 16), (2, 2))),
        "prefix_keys": gaussian(streams_of[3], (PREFIX, HK * HD), 2.0, 12.0, ((0, 256), (1, 2))),
        "prefix_values": gaussian(streams_of[4], (PREFIX, HK * HD), 1.0, 6.0, ((0, 256), (1, 2))),
        "grad_out": gaussian(streams_of[5], (RESPONSES, RESP_LEN, HQ * HD), 1.0, 6.0, ((0, 16), (1, 32))),
        "lengths": draw_lengths(jax.random.fold_in(streams_of[7], 71), 0),
    }


SOFTCAP = 50.0

def reference(queries, keys, values, prefix_keys, prefix_values, grad_out, lengths):
    seq_len = queries.shape[1]
    per_group = HQ // HK
    inv_root = 1.0 / math.sqrt(HD)
    score_factor = 1.0 / (math.sqrt(HD) * SOFTCAP)
    query_pos = jnp.arange(seq_len, dtype=jnp.int32)
    key_pos = jnp.arange(PREFIX + seq_len, dtype=jnp.int32) - PREFIX

    def one_response(which):
        length = lengths[which]
        query_all = queries[which].reshape(seq_len, HQ, HD)
        key_all = jnp.concatenate([prefix_keys, keys[which]], axis=0).reshape(PREFIX + seq_len, HK, HD)
        value_all = jnp.concatenate([prefix_values, values[which]], axis=0).reshape(PREFIX + seq_len, HK, HD)
        is_live = query_pos < length
        grad_rows = jnp.where(is_live[:, None], grad_out[which], jnp.zeros_like(grad_out[which]))
        grad_all = grad_rows.reshape(seq_len, HQ, HD)
        visible = (key_pos[None, :] < 0) | (key_pos[None, :] <= query_pos[:, None]) & (key_pos[None, :] < length)

        def one_head(head_id):
            group_id = head_id // per_group
            query_head = lax.dynamic_index_in_dim(query_all, head_id, 1, keepdims=False)
            key_head = lax.dynamic_index_in_dim(key_all, group_id, 1, keepdims=False)
            value_head = lax.dynamic_index_in_dim(value_all, group_id, 1, keepdims=False)
            grad_head = lax.dynamic_index_in_dim(grad_all, head_id, 1, keepdims=False)
            raw_score = jnp.dot(query_head, key_head.T, preferred_element_type=jnp.float32)
            tangent = jnp.tanh(raw_score * score_factor)
            weights = jnp.where(visible, jnp.exp(SOFTCAP * tangent), 0.0)
            totals = lax.optimization_barrier(jnp.sum(weights, axis=1))
            weighted = jnp.dot(weights.astype(jnp.bfloat16), value_head, preferred_element_type=jnp.float32)
            attn_out = weighted / totals[:, None]
            log_total = jnp.log(totals)
            row_dot = lax.optimization_barrier(jnp.sum(grad_head.astype(jnp.float32) * attn_out, axis=1))
            probs = jnp.where(visible, jnp.exp(SOFTCAP * tangent - log_total[:, None]), 0.0)
            grad_probs = jnp.dot(grad_head, value_head.T, preferred_element_type=jnp.float32)
            grad_score = (probs * (grad_probs - row_dot[:, None]) * (1.0 - tangent * tangent) * inv_root).astype(jnp.bfloat16)
            grad_query = jnp.dot(grad_score, key_head, preferred_element_type=jnp.float32)
            grad_key = jnp.dot(grad_score.T, query_head, preferred_element_type=jnp.float32)
            grad_value = jnp.dot(probs.astype(jnp.bfloat16).T, grad_head, preferred_element_type=jnp.float32)
            return (grad_query, grad_key, grad_value)
        grad_query, grad_key, grad_value = lax.map(one_head, jnp.arange(HQ, dtype=jnp.int32))
        query_out = jnp.transpose(grad_query, (1, 0, 2)).reshape(seq_len, HQ * HD).astype(jnp.bfloat16)
        key_rows = jnp.transpose(grad_key.reshape(HK, per_group, PREFIX + seq_len, HD).sum(axis=1), (1, 0, 2)).reshape(PREFIX + seq_len, HK * HD)
        value_rows = jnp.transpose(grad_value.reshape(HK, per_group, PREFIX + seq_len, HD).sum(axis=1), (1, 0, 2)).reshape(PREFIX + seq_len, HK * HD)
        return (query_out, key_rows[PREFIX:].astype(jnp.bfloat16), value_rows[PREFIX:].astype(jnp.bfloat16), key_rows[:PREFIX], value_rows[:PREFIX])
    query_grads, key_grads, value_grads, prompt_keys, prompt_values = lax.map(one_response, jnp.arange(queries.shape[0], dtype=jnp.int32))
    return (query_grads, key_grads, value_grads, lax.optimization_barrier(jnp.sum(prompt_keys, axis=0)).astype(jnp.bfloat16), lax.optimization_barrier(jnp.sum(prompt_values, axis=0)).astype(jnp.bfloat16))
```

```python
import functools
import math

import jax
import jax.numpy as jnp
from jax import lax
from jax.experimental import pallas as pl
from jax.experimental.pallas import tpu as pltpu
from jax.sharding import PartitionSpec as P

HD = 128
SOFTCAP = 50.0
SCORE_FACTOR = 1.0 / (math.sqrt(HD) * SOFTCAP)
EXP2_FACTOR = SOFTCAP * math.log2(math.e)
INV_ROOT = 1.0 / math.sqrt(HD)

NX, NZL, NY, NZH, NC = 4, 4, 4, 4, 2
NZ = NZL * NZH
BLOCK = 128
HALF = BLOCK // NC
LANES = 512
PROMPT = 512
BASE = [BLOCK * (yb * (yb + 1) // 2) for yb in range(NY)]
SEEN = BLOCK * (NY * (NY + 1) // 2)
OWN, LEFT, RIGHT, FAR = range(4)
MESH = pl.DeviceIdType.MESH

F32 = jnp.float32
BF16 = jnp.bfloat16


def dot(a, b):
    return jnp.dot(a, b, preferred_element_type=F32)


def dot_rows(a, b):
    return lax.dot_general(a, b, (((1,), (1,)), ((), ())), preferred_element_type=F32)


def dot_first(a, b):
    return lax.dot_general(a, b, (((0,), (0,)), ((), ())), preferred_element_type=F32)


def stack_heads(rows):
    return jnp.concatenate([rows[:, h * HD : (h + 1) * HD] for h in range(4)], axis=0)


def kernel(
    len_ref, q_ref, k_ref, v_ref, g_ref, pp_ref,
    gq_ref, gk_ref, gv_ref, gp_ref,
    qb, gb, kz, vz, ka, va, pz, px, pk, pv,
    ep, wp, dp, er, wr, dr,
    tot, rdot, dqt, acc, send_kv, recv_kv, send_z, recv_z,
    send_p, recv_p, part_p, recv_x, tile_p, recv_t, out_q,
    sem_pz, sem_z, sem_q, sem_g, sem_kv, sem_px, sem_py,
    sem_rs, sem_zr, sem_sp, sem_sx, sem_st, sem_oq, sem_own,
):
    resp, pre, core = (lax.axis_index(a) for a in ("resp", "pre", "head"))
    x, zl = resp // NZL, resp % NZL
    y, zh = pre // NZH, pre % NZH
    z = zh * NZL + zl
    left, right, far = (zh + NZH - 1) % NZH, (zh + 1) % NZH, (zh + 2) % NZH
    place_of = [zh, left, right, far]

    def device(x=x, zl=zl, y=y, zh=zh, core=core):
        return {"resp": x * NZL + zl, "pre": y * NZH + zh, "head": core}

    z_partners = [
        ((zl + a) % NZL, (zh + b) % NZH) for b in range(NZH) for a in range(NZL) if a or b
    ]
    y_partners = [(y + a) % NY for a in range(1, NY)]
    yc_partners = [
        ((y + a) % NY, (core + b) % NC) for a in range(NY) for b in range(NC) if a or b
    ]
    x_partners = [(x + a) % NX for a in range(1, NX)]

    started = []

    def send(src, dst, sems, index, to):
        copy = pltpu.make_async_remote_copy(
            src_ref=src,
            dst_ref=dst,
            send_sem=sems.at[(0, *index)],
            recv_sem=sems.at[(1, *index)],
            device_id=to,
            device_id_type=MESH,
        )
        copy.start()
        started.append(copy)
        return copy

    def local(src, dst, index):
        copy = pltpu.make_async_copy(src, dst, sem_own.at[index])
        copy.start()
        return copy

    barrier = pltpu.get_barrier_semaphore()
    greeted = [device(zl=a, zh=b) for a, b in z_partners]
    greeted += [device(y=a, core=b) for a, b in yc_partners]
    greeted += [device(x=a) for a in x_partners]
    for to in greeted:
        pl.semaphore_signal(barrier, inc=1, device_id=to, device_id_type=MESH)
    pl.semaphore_wait(barrier, len(greeted))

    def cols(start, width):
        return pl.ds(pl.multiple_of(start, HD), width)

    def rows(start, count):
        return pl.ds(pl.multiple_of(start, 16), count)

    from_left_k = send(k_ref, kz.at[zh], sem_z, (0,), device(zh=right))
    from_right_v = send(v_ref, vz.at[zh], sem_z, (1,), device(zh=left))
    from_left_v = send(v_ref, vz.at[zh], sem_z, (2,), device(zh=right))
    from_right_k = send(k_ref, kz.at[zh], sem_z, (3,), device(zh=left))

    pieces = [
        send(
            pp_ref,
            pz.at[pl.ds(pl.multiple_of(z * 8, 8), 8)],
            sem_pz,
            (i,),
            device(zl=a, zh=b),
        )
        for i, (a, b) in enumerate(z_partners)
    ]
    pz[pl.ds(pl.multiple_of(z * 8, 8), 8), :] = pp_ref[...]

    queries_in = [
        send(q_ref.at[:, cols(a * LANES, LANES)], qb.at[y], sem_q, (i,), device(y=a))
        for i, a in enumerate(y_partners)
    ]
    own = [local(q_ref.at[:, cols(y * LANES, LANES)], qb.at[y], 0)]

    def spread(step, key_ref, value_ref):
        at = pl.ds(pl.multiple_of(y * BLOCK, BLOCK), BLOCK)
        copies = []
        for i, a in enumerate(y_partners):
            group = cols((a // 2) * HD, HD)
            to = device(y=a)
            zs = place_of[step]
            copies.append(send(key_ref.at[:, group], ka.at[zs, at], sem_kv, (step, 0, i), to))
            copies.append(send(value_ref.at[:, group], va.at[zs, at], sem_kv, (step, 1, i), to))
        group = cols((y // 2) * HD, HD)
        copies_own = [
            local(key_ref.at[:, group], ka.at[place_of[step], at], 2 + 2 * step),
            local(value_ref.at[:, group], va.at[place_of[step], at], 3 + 2 * step),
        ]
        return copies, copies_own

    block_in = [spread(OWN, k_ref, v_ref), None, None, None]
    grads_in = [
        send(
            g_ref.at[:, cols(b * (NY * LANES) + a * LANES, LANES)],
            gb.at[y, rows(core * HALF, HALF)],
            sem_g,
            (i,),
            device(y=a, core=b),
        )
        for i, (a, b) in enumerate(yc_partners)
    ]
    own.append(
        local(
            g_ref.at[:, cols(core * (NY * LANES) + y * LANES, LANES)],
            gb.at[y, rows(core * HALF, HALF)],
            1,
        )
    )

    for copy in pieces:
        copy.wait_recv()
    mine_x = pl.ds(pl.multiple_of(x * 32, 32), 32)
    for t in range(4):
        for k in range(2):
            piece = pz[pl.ds(t * 2 + k, NZ, stride=8), :].astype(BF16)
            px[t, pl.ds(pl.multiple_of(x * 32 + k * 16, 16), 16), :] = piece
    prompt_x = [
        send(px.at[:, mine_x], px.at[:, mine_x], sem_px, (i,), device(x=a))
        for i, a in enumerate(x_partners)
    ]

    from_left_k.wait_recv()
    far_k = send(kz.at[left], kz.at[left], sem_z, (4,), device(zh=right))
    from_right_v.wait_recv()
    far_v = send(vz.at[right], vz.at[right], sem_z, (5,), device(zh=left))

    for copy in prompt_x:
        copy.wait_recv()
    mine_y = pl.ds(pl.multiple_of(y * BLOCK, BLOCK), BLOCK)
    prompt_y = []
    for i, a in enumerate(y_partners):
        prompt_y.append(send(px.at[a // 2], pk.at[mine_y], sem_py, (0, i), device(y=a)))
        prompt_y.append(send(px.at[2 + a // 2], pv.at[mine_y], sem_py, (1, i), device(y=a)))
    own_prompt = [
        local(px.at[y // 2], pk.at[mine_y], 10),
        local(px.at[2 + y // 2], pv.at[mine_y], 11),
    ]

    for copy in queries_in + grads_in:
        copy.wait_recv()
    for copy in own:
        copy.wait()
    length = len_ref[0]
    for yb in range(NY):
        pos = lax.broadcasted_iota(jnp.int32, (BLOCK, LANES), 0) + (yb * NZH + zh) * BLOCK
        gb[yb] = jnp.where(pos < length, gb[yb].astype(F32), 0.0).astype(BF16)
        tot[yb] = jnp.zeros((8, LANES), F32)
        rdot[yb] = jnp.zeros((8, LANES), F32)
        dqt[yb] = jnp.zeros((HD, LANES), F32)

    key_at = lax.broadcasted_iota(jnp.int32, (BLOCK, LANES), 0)
    query_at = lax.broadcasted_iota(jnp.int32, (BLOCK, LANES), 1) % BLOCK
    gap = key_at - query_at

    def first_pass(yb, keys, values, count, e_ref, w_ref, d_ref, base, limit):
        queries, grads = stack_heads(qb[yb]), stack_heads(gb[yb])
        total, row_dot = tot[yb], rdot[yb]
        for c in range(count):
            at = pl.ds(c * BLOCK, BLOCK)
            score = dot_rows(keys[at, :], queries)
            grad_prob = dot_rows(values[at, :], grads)
            tangent = jnp.tanh(score * SCORE_FACTOR)
            weight = jnp.exp2(tangent * EXP2_FACTOR)
            if limit is not None and c == count - 1:
                weight = jnp.where(gap <= limit, weight, 0.0)
            slope = weight * (1.0 - tangent * tangent)
            total = total + weight.reshape(BLOCK // 8, 8, LANES).sum(0)
            row_dot = row_dot + (weight * grad_prob).reshape(BLOCK // 8, 8, LANES).sum(0)
            to = pl.ds(base + c * BLOCK, BLOCK)
            e_ref[to, :] = weight.astype(BF16)
            w_ref[to, :] = slope.astype(BF16)
            d_ref[to, :] = grad_prob.astype(BF16)
        tot[yb] = total
        rdot[yb] = row_dot

    def response_first(step):
        zs = place_of[step]
        limit = (zh - zs) * BLOCK
        copies, copies_own = block_in[step]
        for copy in copies:
            copy.wait_recv()
        for copy in copies_own:
            copy.wait()
        for yb in range(NY):
            first_pass(
                yb, ka.at[zs], va.at[zs], yb + 1,
                er.at[step], wr.at[step], dr.at[step], BASE[yb], limit,
            )

    response_first(OWN)
    from_left_v.wait_recv()
    block_in[LEFT] = spread(LEFT, kz.at[left], vz.at[left])
    from_right_k.wait_recv()
    block_in[RIGHT] = spread(RIGHT, kz.at[right], vz.at[right])

    for copy in prompt_y:
        copy.wait_recv()
    for copy in own_prompt:
        copy.wait()
    for yb in range(NY):
        first_pass(yb, pk, pv, PROMPT // BLOCK, ep.at[yb], wp.at[yb], dp.at[yb], 0, None)

    response_first(LEFT)
    far_k.wait_recv()
    far_v.wait_recv()
    block_in[FAR] = spread(FAR, kz.at[far], vz.at[far])
    response_first(RIGHT)
    response_first(FAR)

    for yb in range(NY):
        total = jnp.sum(tot[yb], axis=0, keepdims=True)
        row_dot = jnp.sum(rdot[yb], axis=0, keepdims=True)
        inverse = 1.0 / total
        tot[yb] = jnp.broadcast_to(inverse, (8, LANES))
        rdot[yb] = jnp.broadcast_to(row_dot * inverse, (8, LANES))

    def second_pass(yb, keys, count, e_ref, w_ref, d_ref, base, fresh):
        queries, grads = stack_heads(qb[yb]), stack_heads(gb[yb])
        inverse = tot[yb, 0:1, :]
        inverse_root = inverse * INV_ROOT
        row_dot = rdot[yb, 0:1, :]
        query_grad = dqt[yb]
        for c in range(count):
            at = pl.ds(base + c * BLOCK, BLOCK)
            to = pl.ds(c * BLOCK, BLOCK)
            prob = (e_ref[at, :].astype(F32) * inverse).astype(BF16)
            grad_score = (
                (w_ref[at, :].astype(F32) * inverse_root) * (d_ref[at, :].astype(F32) - row_dot)
            ).astype(BF16)
            key_grad = dot(grad_score, queries)
            value_grad = dot(prob, grads)
            query_grad = query_grad + dot_first(keys[to, :], grad_score)
            if fresh(c):
                acc[0, to, :] = key_grad
                acc[1, to, :] = value_grad
            else:
                acc[0, to, :] += key_grad
                acc[1, to, :] += value_grad
        dqt[yb] = query_grad

    partials = [None] * 4

    def response_second(step):
        for yb in range(NY):
            second_pass(
                yb, ka.at[place_of[step]], yb + 1,
                er.at[step], wr.at[step], dr.at[step], BASE[yb], lambda c, yb=yb: c == yb,
            )
        send_kv[step] = acc[...].astype(BF16)
        partials[step] = [
            send(
                send_kv.at[step, :, rows(a * BLOCK + b * HALF, HALF)],
                recv_kv.at[step, y * NC + core],
                sem_rs,
                (step, i),
                device(y=a, core=b),
            )
            for i, (a, b) in enumerate(yc_partners)
        ]
        recv_kv[step, y * NC + core] = send_kv[step, :, rows(y * BLOCK + core * HALF, HALF), :]

    def summed(step, which):
        groups = []
        for c in range(NC):
            for g in range(2):
                first = recv_kv[step, (2 * g) * NC + c, which].astype(F32)
                second = recv_kv[step, (2 * g + 1) * NC + c, which].astype(F32)
                groups.append(first + second)
        return jnp.concatenate(groups, axis=1)

    def collect(step):
        for copy in partials[step]:
            copy.wait_recv()

    response_second(FAR)
    response_second(LEFT)
    collect(FAR)
    for which in range(2):
        send_z[FAR, which] = summed(FAR, which).astype(BF16)
    far_key = send(send_z.at[FAR, 0], recv_z.at[0], sem_zr, (0,), device(zh=right))
    far_value = send(send_z.at[FAR, 1], recv_z.at[1], sem_zr, (1,), device(zh=left))

    response_second(RIGHT)
    collect(LEFT)
    send_z[LEFT, 0] = summed(LEFT, 0).astype(BF16)
    key_right = send(send_z.at[LEFT, 0], recv_z.at[4], sem_zr, (4,), device(zh=left))

    for yb in range(NY):
        second_pass(
            yb, pk, PROMPT // BLOCK, ep.at[yb], wp.at[yb], dp.at[yb], 0, lambda c, yb=yb: yb == 0
        )
    send_p[...] = acc[...].astype(BF16)
    prompt_back = [
        send(
            send_p.at[:, pl.ds(pl.multiple_of(a * BLOCK, BLOCK), BLOCK)],
            recv_p.at[y],
            sem_sp,
            (i,),
            device(y=a),
        )
        for i, a in enumerate(y_partners)
    ]
    recv_p[y] = send_p[:, pl.ds(pl.multiple_of(y * BLOCK, BLOCK), BLOCK), :]

    collect(RIGHT)
    send_z[RIGHT, 1] = summed(RIGHT, 1).astype(BF16)
    value_left = send(send_z.at[RIGHT, 1], recv_z.at[3], sem_zr, (3,), device(zh=right))
    far_key.wait_recv()
    send_z[RIGHT, 0] = (summed(RIGHT, 0) + recv_z[0].astype(F32)).astype(BF16)
    key_left = send(send_z.at[RIGHT, 0], recv_z.at[2], sem_zr, (2,), device(zh=right))
    far_value.wait_recv()
    send_z[LEFT, 1] = (summed(LEFT, 1) + recv_z[1].astype(F32)).astype(BF16)
    value_right = send(send_z.at[LEFT, 1], recv_z.at[5], sem_zr, (5,), device(zh=left))

    response_second(OWN)

    for yb in range(NY):
        for h in range(4):
            at = pl.ds(h * HD, HD)
            out_q[yb, :, at] = dqt[yb, :, at].T.astype(BF16)
    mine = cols(core * (NY * LANES) + y * LANES, LANES)
    query_back = [
        send(
            out_q.at[a, rows(b * HALF, HALF)],
            gq_ref.at[:, mine],
            sem_oq,
            (i,),
            device(y=a, core=b),
        )
        for i, (a, b) in enumerate(yc_partners)
    ]
    own_back = local(out_q.at[y, rows(core * HALF, HALF)], gq_ref.at[:, mine], 12)

    for copy in prompt_back:
        copy.wait_recv()
    for which in range(2):
        for g in range(2):
            part_p[2 * which + g] = recv_p[2 * g, which].astype(F32) + recv_p[
                2 * g + 1, which
            ].astype(F32)
    prompt_x_back = [
        send(
            part_p.at[:, pl.ds(pl.multiple_of(a * 32, 32), 32)],
            recv_x.at[i],
            sem_sx,
            (i,),
            device(x=a),
        )
        for i, a in enumerate(x_partners)
    ]
    for copy in prompt_x_back:
        copy.wait_recv()
    for t in range(4):
        part = part_p[t, mine_x, :]
        for i in range(NX - 1):
            part = part + recv_x[i, t]
        for k in range(2):
            tile_p[pl.ds(t * 2 + k, NZ, stride=8), :] = part[k * 16 : (k + 1) * 16]
    tiles_back = [
        send(
            tile_p.at[pl.ds(pl.multiple_of((b * NZL + a) * 8, 8), 8)],
            recv_t.at[i],
            sem_st,
            (i,),
            device(zl=a, zh=b),
        )
        for i, (a, b) in enumerate(z_partners)
    ]

    collect(OWN)
    key_left.wait_recv()
    key_right.wait_recv()
    gk_ref[...] = (summed(OWN, 0) + recv_z[2].astype(F32) + recv_z[4].astype(F32)).astype(BF16)
    value_left.wait_recv()
    value_right.wait_recv()
    gv_ref[...] = (summed(OWN, 1) + recv_z[3].astype(F32) + recv_z[5].astype(F32)).astype(BF16)

    for copy in tiles_back:
        copy.wait_recv()
    tile = tile_p[pl.ds(pl.multiple_of(z * 8, 8), 8), :]
    for i in range(NZ - 1):
        tile = tile + recv_t[i]
    gp_ref[...] = tile

    for copy in query_back:
        copy.wait_recv()
    own_back.wait()
    for copy in started:
        copy.wait_send()


def shards(queries, keys, values, prefix_keys, prefix_values, grad_out, lengths):
    def by_group(prompt_rows):
        return prompt_rows.reshape(2, 2, HD).transpose(1, 0, 2).reshape(4, HD)

    prompt = jnp.concatenate([by_group(prefix_keys), by_group(prefix_values)], axis=0).astype(F32)
    vmem = pl.BlockSpec(memory_space=pltpu.VMEM)
    anywhere = pl.BlockSpec(memory_space=pl.ANY)
    smem = pl.BlockSpec(memory_space=pltpu.SMEM)

    def sems(*dims):
        return pltpu.SemaphoreType.DMA((2, *dims))

    grad_queries, grad_keys, grad_values, grad_prompt = pl.pallas_call(
        kernel,
        out_shape=(
            jax.ShapeDtypeStruct((HALF, NC * NY * LANES), BF16),
            jax.ShapeDtypeStruct((HALF, 4 * HD), BF16),
            jax.ShapeDtypeStruct((HALF, 4 * HD), BF16),
            jax.ShapeDtypeStruct((8, HD), F32),
        ),
        in_specs=[smem, anywhere, anywhere, anywhere, anywhere, vmem],
        out_specs=(anywhere, vmem, vmem, vmem),
        scratch_shapes=[
            pltpu.VMEM((NY, BLOCK, LANES), BF16),
            pltpu.VMEM((NY, BLOCK, LANES), BF16),
            pltpu.VMEM((NZH, BLOCK, 2 * HD), BF16),
            pltpu.VMEM((NZH, BLOCK, 2 * HD), BF16),
            pltpu.VMEM((NZH, NY * BLOCK, HD), BF16),
            pltpu.VMEM((NZH, NY * BLOCK, HD), BF16),
            pltpu.VMEM((NZ * 8, HD), F32),
            pltpu.VMEM((4, NX * 32, HD), BF16),
            pltpu.VMEM((PROMPT, HD), BF16),
            pltpu.VMEM((PROMPT, HD), BF16),
            pltpu.VMEM((NY, PROMPT, LANES), BF16),
            pltpu.VMEM((NY, PROMPT, LANES), BF16),
            pltpu.VMEM((NY, PROMPT, LANES), BF16),
            pltpu.VMEM((NZH, SEEN, LANES), BF16),
            pltpu.VMEM((NZH, SEEN, LANES), BF16),
            pltpu.VMEM((NZH, SEEN, LANES), BF16),
            pltpu.VMEM((NY, 8, LANES), F32),
            pltpu.VMEM((NY, 8, LANES), F32),
            pltpu.VMEM((NY, HD, LANES), F32),
            pltpu.VMEM((2, NY * BLOCK, HD), F32),
            pltpu.VMEM((NZH, 2, NY * BLOCK, HD), BF16),
            pltpu.VMEM((NZH, NY * NC, 2, HALF, HD), BF16),
            pltpu.VMEM((NZH, 2, HALF, 4 * HD), BF16),
            pltpu.VMEM((6, HALF, 4 * HD), BF16),
            pltpu.VMEM((2, PROMPT, HD), BF16),
            pltpu.VMEM((NY, 2, BLOCK, HD), BF16),
            pltpu.VMEM((4, NX * 32, HD), F32),
            pltpu.VMEM((NX - 1, 4, 32, HD), F32),
            pltpu.VMEM((NZ * 8, HD), F32),
            pltpu.VMEM((NZ - 1, 8, HD), F32),
            pltpu.VMEM((NY, BLOCK, LANES), BF16),
            sems(NZ - 1),
            sems(6),
            sems(NY - 1),
            sems(NY * NC - 1),
            sems(NZH, 2, NY - 1),
            sems(NX - 1),
            sems(2, NY - 1),
            sems(NZH, NY * NC - 1),
            sems(6),
            sems(NY - 1),
            sems(NX - 1),
            sems(NZ - 1),
            sems(NY * NC - 1),
            pltpu.SemaphoreType.DMA((13,)),
        ],
        compiler_params=pltpu.CompilerParams(
            collective_id=0, has_side_effects=True, vmem_limit_bytes=48 * 2**20
        ),
        name="attention_grads",
    )(lengths, queries[0], keys[0], values[0], grad_out[0], prompt)

    def rows_of(block):
        return block.reshape(2, 2, HD).transpose(1, 0, 2).reshape(2, 2 * HD).astype(BF16)

    return (
        grad_queries[None],
        grad_keys[None],
        grad_values[None],
        rows_of(grad_prompt[:4]),
        rows_of(grad_prompt[4:]),
    )


def solution(mesh):
    in_specs = (
        P("resp", "pre", "head"),
        P("resp", "pre", "head"),
        P("resp", "pre", "head"),
        P(("resp", "pre"), "head"),
        P(("resp", "pre"), "head"),
        P("resp", ("pre", "head"), None),
        P("resp"),
    )
    out_specs = (
        P("resp", ("pre", "head"), None),
        P("resp", ("pre", "head"), None),
        P("resp", ("pre", "head"), None),
        P(("resp", "pre"), "head"),
        P(("resp", "pre"), "head"),
    )
    return jax.shard_map(shards, mesh=mesh, in_specs=in_specs, out_specs=out_specs, check_vma=False)
```

```python
import functools
import math

import jax
import jax.numpy as jnp
from jax import lax
from jax.experimental import pallas as pl
from jax.experimental.pallas import tpu as pltpu
from jax.sharding import PartitionSpec as P

HD = 128
SOFTCAP = 50.0
SCORE_FACTOR = 1.0 / (math.sqrt(HD) * SOFTCAP)
EXP2_FACTOR = SOFTCAP * math.log2(math.e)
INV_ROOT = 1.0 / math.sqrt(HD)

NX, NZL, NY, NZH, NC = 4, 4, 4, 4, 2
NZ = NZL * NZH
BLOCK = 128
HALF = BLOCK // NC
LANES = 512
PROMPT = 512
VMEM_BYTES = 62 * 2**20
BASE = [BLOCK * (yb * (yb + 1) // 2) for yb in range(NY)]
SEEN = BLOCK * (NY * (NY + 1) // 2)
OWN, LEFT, RIGHT, FAR = range(4)
MESH = pl.DeviceIdType.MESH

F32 = jnp.float32
BF16 = jnp.bfloat16


def dot(a, b):
    return jnp.dot(a, b, preferred_element_type=F32)


def dot_rows(a, b):
    return lax.dot_general(a, b, (((1,), (1,)), ((), ())), preferred_element_type=F32)


def dot_first(a, b):
    return lax.dot_general(a, b, (((0,), (0,)), ((), ())), preferred_element_type=F32)


def stack_heads(rows):
    return jnp.concatenate([rows[:, h * HD : (h + 1) * HD] for h in range(4)], axis=0)


def kernel(
    len_ref, q_ref, k_ref, v_ref, g_ref, pk_ref, pv_ref,
    gq_ref, gk_ref, gv_ref, gpk_ref, gpv_ref,
    qb, gb, kvz, kva, pz, px, pkv,
    ep, wp, dp, er, wr, dr,
    tot, rdot, dqt, acc, other, send_kv, recv_kv, send_z, recv_z,
    send_p, part_p, recv_x, tile_p, recv_t, out_q,
    sem_pz, sem_z, sem_qs, sem_qr, sem_g, sem_kvs, sem_kvr, sem_ex, sem_px, sem_pys, sem_pyr,
    sem_rx, sem_rs, sem_zr, sem_sps, sem_spr, sem_sx, sem_st, sem_oq, sem_own,
):
    resp, pre, core = (lax.axis_index(a) for a in ("resp", "pre", "head"))
    x, zl = resp // NZL, resp % NZL
    y, zh = pre // NZH, pre % NZH
    z = zh * NZL + zl
    left, right, far = (zh + NZH - 1) % NZH, (zh + 1) % NZH, (zh + 2) % NZH
    place_of = [zh, left, right, far]

    def device(x=x, zl=zl, y=y, zh=zh, core=core):
        return {"resp": x * NZL + zl, "pre": y * NZH + zh, "head": core}

    z_partners = [
        ((zl + a) % NZL, (zh + b) % NZH) for b in range(NZH) for a in range(NZL) if a or b
    ]
    yc_partners = [
        ((y + a) % NY, (core + b) % NC) for a in range(NY) for b in range(NC) if a or b
    ]
    x_partners = [(x + a) % NX for a in range(1, NX)]

    started = []

    def send(src, dst, sems, index, to):
        copy = pltpu.make_async_remote_copy(
            src_ref=src,
            dst_ref=dst,
            send_sem=sems.at[(0, *index)],
            recv_sem=sems.at[(1, *index)],
            device_id=to,
            device_id_type=MESH,
        )
        copy.start()
        started.append(copy)
        return copy

    conditional = []

    def deliver(src, dst, send_sem, recv_sem, to, here):
        copy = pltpu.make_async_remote_copy(
            src_ref=src,
            dst_ref=dst,
            send_sem=send_sem,
            recv_sem=recv_sem,
            device_id=to,
            device_id_type=MESH,
        )

        @pl.when(here)
        def _():
            pltpu.make_async_copy(src, dst, recv_sem).start()

        @pl.when(jnp.logical_not(here))
        def _():
            copy.start()

        conditional.append((copy, here))

    def delivered(dst, recv_sem):
        pltpu.make_async_copy(dst, dst, recv_sem).wait()

    def local(src, dst, index):
        copy = pltpu.make_async_copy(src, dst, sem_own.at[index])
        copy.start()
        return copy

    def cols(start, width):
        return pl.ds(pl.multiple_of(start, HD), width)

    def rows(start, count):
        return pl.ds(pl.multiple_of(start, 16), count)

    packed = [
        local(ref.at[:, pl.ds(g * HD, HD)], kvz.at[zh, g, which], 2 + 2 * g + which)
        for g in range(2)
        for which, ref in enumerate((k_ref, v_ref))
    ]
    mine_g = cols(y * (NC * LANES) + core * LANES, LANES)
    own_grads = local(g_ref.at[:, mine_g], gb.at[y, rows(core * HALF, HALF)], 1)
    mine_z = pl.ds(pl.multiple_of(z * 8, 8), 8)
    pz[mine_z, :] = jnp.concatenate(
        [
            ref[:, g * HD : (g + 1) * HD].astype(F32)
            for ref in (pk_ref, pv_ref)
            for g in range(2)
        ],
        axis=0,
    )

    barrier = pltpu.get_barrier_semaphore()
    greeted = [device(zl=a, zh=b) for a, b in z_partners]
    greeted += [device(y=a, core=b) for a, b in yc_partners]
    greeted += [device(x=a) for a in x_partners]
    for to in greeted:
        pl.semaphore_signal(barrier, inc=1, device_id=to, device_id_type=MESH)
    pl.semaphore_wait(barrier, len(greeted))

    pieces = [
        send(pz.at[mine_z], pz.at[mine_z], sem_pz, (i,), device(zl=a, zh=b))
        for i, (a, b) in enumerate(z_partners)
    ]

    for copy in packed:
        copy.wait()
    left_first = send(kvz.at[zh, 0], kvz.at[zh, 0], sem_z, (0,), device(zh=right))
    right_first = send(kvz.at[zh, 1], kvz.at[zh, 1], sem_z, (1,), device(zh=left))

    takers = [
        (j, b, 2 * core + j, jnp.logical_and(y == 2 * core + j, core == b))
        for j in range(2)
        for b in range(NC)
    ]

    def spread(step):
        zs = place_of[step]
        for i, (j, b, a, here) in enumerate(takers):
            deliver(
                kvz.at[zs, j, b], kva.at[zs, b, y],
                sem_kvs.at[step, i], sem_kvr.at[step, y], device(y=a, core=b), here,
            )

    def swap(step):
        zs = place_of[step]
        for a in range(NY):
            delivered(kva.at[zs, core, a], sem_kvr.at[step, a])
        return send(kva.at[zs, core], kva.at[zs, core], sem_ex, (step,), device(core=1 - core))

    for i, (j, b, a, here) in enumerate(takers):
        deliver(
            q_ref.at[:, pl.ds((j * NC + b) * LANES, LANES)], qb.at[y],
            sem_qs.at[i], sem_qr.at[y], device(y=a, core=b), here,
        )
    spread(OWN)
    grads_in = [
        send(
            g_ref.at[:, cols(a * (NC * LANES) + b * LANES, LANES)],
            gb.at[y, rows(core * HALF, HALF)],
            sem_g,
            (i,),
            device(y=a, core=b),
        )
        for i, (a, b) in enumerate(yc_partners)
    ]
    left_second = send(kvz.at[zh, 1], kvz.at[zh, 1], sem_z, (2,), device(zh=right))
    right_second = send(kvz.at[zh, 0], kvz.at[zh, 0], sem_z, (3,), device(zh=left))

    for copy in pieces:
        copy.wait_recv()
    mine_x = pl.ds(pl.multiple_of(x * 32, 32), 32)
    for t in range(4):
        for k in range(2):
            piece = pz[pl.ds(t * 2 + k, NZ, stride=8), :].astype(BF16)
            px[t, pl.ds(pl.multiple_of(x * 32 + k * 16, 16), 16), :] = piece
    prompt_x = [
        send(px.at[:, mine_x], px.at[:, mine_x], sem_px, (i,), device(x=a))
        for i, a in enumerate(x_partners)
    ]

    left_first.wait_recv()
    far_0 = send(kvz.at[left, 0], kvz.at[left, 0], sem_z, (4,), device(zh=right))
    right_first.wait_recv()
    far_1 = send(kvz.at[right, 1], kvz.at[right, 1], sem_z, (5,), device(zh=left))

    swapped = [swap(OWN), None, None, None]
    for copy in prompt_x:
        copy.wait_recv()
    mine_y = pl.ds(pl.multiple_of(y * BLOCK, BLOCK), BLOCK)
    for i, (j, b, a, here) in enumerate(takers):
        deliver(
            px.at[2 * b + j], pkv.at[b, mine_y],
            sem_pys.at[i], sem_pyr.at[y], device(y=a, core=b), here,
        )

    left_second.wait_recv()
    spread(LEFT)
    right_second.wait_recv()
    spread(RIGHT)

    for a in range(NY):
        delivered(qb.at[a], sem_qr.at[a])
    for copy in grads_in:
        copy.wait_recv()
    own_grads.wait()
    length = len_ref[0]
    for yb in range(NY):
        pos = lax.broadcasted_iota(jnp.int32, (BLOCK, LANES), 0) + (yb * NZH + zh) * BLOCK
        gb[yb] = jnp.where(pos < length, gb[yb].astype(F32), 0.0).astype(BF16)
        tot[yb] = jnp.zeros((8, LANES), F32)
        rdot[yb] = jnp.zeros((8, LANES), F32)
        dqt[yb] = jnp.zeros((HD, LANES), F32)

    key_at = lax.broadcasted_iota(jnp.int32, (BLOCK, LANES), 0)
    query_at = lax.broadcasted_iota(jnp.int32, (BLOCK, LANES), 1) % BLOCK
    gap = key_at - query_at

    def response_keys(step):
        return lambda c: kva[place_of[step], 0, c]

    def response_values(step):
        return lambda c: kva[place_of[step], 1, c]

    def prompt_keys(c):
        return pkv[0, pl.ds(c * BLOCK, BLOCK), :]

    def prompt_values(c):
        return pkv[1, pl.ds(c * BLOCK, BLOCK), :]

    def first_pass(yb, keys, values, count, e_ref, w_ref, d_ref, base, limit):
        queries, grads = stack_heads(qb[yb]), stack_heads(gb[yb])
        total, row_dot = tot[yb], rdot[yb]
        for c in range(count):
            score = dot_rows(keys(c), queries)
            grad_prob = dot_rows(values(c), grads)
            tangent = jnp.tanh(score * SCORE_FACTOR)
            weight = jnp.exp2(tangent * EXP2_FACTOR)
            if limit is not None and c == count - 1:
                weight = jnp.where(gap <= limit, weight, 0.0)
            slope = weight * (1.0 - tangent * tangent)
            total = total + weight.reshape(BLOCK // 8, 8, LANES).sum(0)
            row_dot = row_dot + (weight * grad_prob).reshape(BLOCK // 8, 8, LANES).sum(0)
            to = pl.ds(base + c * BLOCK, BLOCK)
            e_ref[to, :] = weight.astype(BF16)
            w_ref[to, :] = slope.astype(BF16)
            d_ref[to, :] = grad_prob.astype(BF16)
        tot[yb] = total
        rdot[yb] = row_dot

    def response_first(step):
        zs = place_of[step]
        limit = (zh - zs) * BLOCK
        swapped[step].wait_recv()
        for yb in range(NY):
            first_pass(
                yb, response_keys(step), response_values(step), yb + 1,
                er.at[step], wr.at[step], dr.at[step], BASE[yb], limit,
            )

    response_first(OWN)
    for a in range(NY):
        delivered(pkv.at[core, pl.ds(a * BLOCK, BLOCK)], sem_pyr.at[a])
    swapped_prompt = send(pkv.at[core], pkv.at[core], sem_ex, (4,), device(core=1 - core))
    swapped[LEFT] = swap(LEFT)
    swapped[RIGHT] = swap(RIGHT)

    swapped_prompt.wait_recv()
    for yb in range(NY):
        first_pass(
            yb, prompt_keys, prompt_values, PROMPT // BLOCK,
            ep.at[yb], wp.at[yb], dp.at[yb], 0, None,
        )

    far_0.wait_recv()
    far_1.wait_recv()
    spread(FAR)
    response_first(LEFT)
    response_first(RIGHT)
    swapped[FAR] = swap(FAR)
    response_first(FAR)

    for yb in range(NY):
        total = jnp.sum(tot[yb], axis=0, keepdims=True)
        row_dot = jnp.sum(rdot[yb], axis=0, keepdims=True)
        inverse = 1.0 / total
        tot[yb] = jnp.broadcast_to(inverse, (8, LANES))
        rdot[yb] = jnp.broadcast_to(row_dot * inverse, (8, LANES))

    def second_pass(yb, keys, count, e_ref, w_ref, d_ref, base, fresh, acc):
        queries, grads = stack_heads(qb[yb]), stack_heads(gb[yb])
        inverse = tot[yb, 0:1, :]
        inverse_root = inverse * INV_ROOT
        row_dot = rdot[yb, 0:1, :]
        query_grad = dqt[yb]
        for c in range(count):
            at = pl.ds(base + c * BLOCK, BLOCK)
            to = pl.ds(c * BLOCK, BLOCK)
            prob = (e_ref[at, :].astype(F32) * inverse).astype(BF16)
            grad_score = (
                (w_ref[at, :].astype(F32) * inverse_root) * (d_ref[at, :].astype(F32) - row_dot)
            ).astype(BF16)
            key_grad = dot(grad_score, queries)
            value_grad = dot(prob, grads)
            query_grad = query_grad + dot_first(keys(c), grad_score)
            if fresh(c):
                acc[0, to, :] = key_grad
                acc[1, to, :] = value_grad
            else:
                acc[0, to, :] += key_grad
                acc[1, to, :] += value_grad
        dqt[yb] = query_grad

    def trade(step):
        return send(acc.at[step, 1 - core], other.at[step], sem_rx, (step,), device(core=1 - core))

    partials = [None] * 4
    traded = [None] * 5

    def response_second(step):
        for yb in range(NY):
            second_pass(
                yb, response_keys(step), yb + 1,
                er.at[step], wr.at[step], dr.at[step], BASE[yb], lambda c, yb=yb: c == yb,
                acc.at[step],
            )
        traded[step] = trade(step)

    def hand_out(step):
        traded[step].wait_recv()
        send_kv[step] = (acc[step, core] + other[step]).astype(BF16)
        partials[step] = [
            send(
                send_kv.at[step, rows(a * BLOCK + b * HALF, HALF)],
                recv_kv.at[step, core, y],
                sem_rs,
                (step, i),
                device(y=a, core=b),
            )
            for i, (a, b) in enumerate(yc_partners)
        ]
        recv_kv[step, core, y] = send_kv[step, rows(y * BLOCK + core * HALF, HALF), :]

    def collect(step):
        for copy in partials[step]:
            copy.wait_recv()

    response_second(FAR)

    for yb in range(NY):
        second_pass(
            yb, prompt_keys, PROMPT // BLOCK, ep.at[yb], wp.at[yb], dp.at[yb], 0,
            lambda c, yb=yb: yb == 0, acc.at[4],
        )
    traded[4] = trade(4)
    hand_out(FAR)
    response_second(LEFT)

    traded[4].wait_recv()
    send_p[...] = acc[4, core] + other[4]
    for a in range(NY):
        deliver(
            send_p.at[pl.ds(a * BLOCK, BLOCK)], part_p.at[2 * core + y % 2],
            sem_sps.at[a], sem_spr.at[2 * core + y % 2], device(y=a, core=y // 2),
            jnp.logical_and(y == a, core == y // 2),
        )
    collect(FAR)
    far_key = send(recv_kv.at[FAR, 0], recv_z.at[0], sem_zr, (0,), device(zh=right))
    far_value = send(recv_kv.at[FAR, 1], recv_z.at[1], sem_zr, (1,), device(zh=left))
    hand_out(LEFT)
    response_second(RIGHT)

    for t in range(4):
        delivered(part_p.at[t], sem_spr.at[t])
    prompt_x_back = [
        send(
            part_p.at[:, pl.ds(pl.multiple_of(a * 32, 32), 32)],
            recv_x.at[i],
            sem_sx,
            (i,),
            device(x=a),
        )
        for i, a in enumerate(x_partners)
    ]
    collect(LEFT)
    key_right = send(recv_kv.at[LEFT, 0], recv_z.at[4], sem_zr, (4,), device(zh=left))
    hand_out(RIGHT)
    response_second(OWN)

    for yb in range(NY):
        for h in range(4):
            at = pl.ds(h * HD, HD)
            out_q[yb, :, at] = dqt[yb, :, at].T.astype(BF16)
    query_back = [
        send(
            out_q.at[a, rows(b * HALF, HALF)],
            gq_ref.at[:, mine_g],
            sem_oq,
            (i,),
            device(y=a, core=b),
        )
        for i, (a, b) in enumerate(yc_partners)
    ]
    own_back = local(out_q.at[y, rows(core * HALF, HALF)], gq_ref.at[:, mine_g], 12)

    for copy in prompt_x_back:
        copy.wait_recv()
    for t in range(4):
        part = part_p[t, mine_x, :]
        for i in range(NX - 1):
            part = part + recv_x[i, t]
        for k in range(2):
            tile_p[pl.ds(t * 2 + k, NZ, stride=8), :] = part[k * 16 : (k + 1) * 16]
    tiles_back = [
        send(
            tile_p.at[pl.ds(pl.multiple_of((b * NZL + a) * 8, 8), 8)],
            recv_t.at[i],
            sem_st,
            (i,),
            device(zl=a, zh=b),
        )
        for i, (a, b) in enumerate(z_partners)
    ]

    collect(RIGHT)
    value_left = send(recv_kv.at[RIGHT, 1], recv_z.at[3], sem_zr, (3,), device(zh=right))
    hand_out(OWN)
    far_key.wait_recv()
    send_z[0] = (recv_kv[RIGHT, 0].astype(F32) + recv_z[0].astype(F32)).astype(BF16)
    key_left = send(send_z.at[0], recv_z.at[2], sem_zr, (2,), device(zh=right))
    far_value.wait_recv()
    send_z[1] = (recv_kv[LEFT, 1].astype(F32) + recv_z[1].astype(F32)).astype(BF16)
    value_right = send(send_z.at[1], recv_z.at[5], sem_zr, (5,), device(zh=left))

    collect(OWN)
    key_left.wait_recv()
    key_right.wait_recv()
    value_left.wait_recv()
    value_right.wait_recv()
    for which, ref, first, second in ((0, gk_ref, 2, 4), (1, gv_ref, 3, 5)):
        for a in range(NY):
            total = recv_kv[OWN, which, a].astype(F32) + recv_z[first, a].astype(F32)
            ref[:, pl.ds(a * HD, HD)] = (total + recv_z[second, a].astype(F32)).astype(BF16)

    for copy in tiles_back:
        copy.wait_recv()
    tile = tile_p[mine_z, :]
    for i in range(NZ - 1):
        tile = tile + recv_t[i]
    for which, ref in enumerate((gpk_ref, gpv_ref)):
        for g in range(2):
            at = 4 * which + 2 * g
            ref[:, pl.ds(g * HD, HD)] = tile[at : at + 2].astype(BF16)

    for copy in query_back:
        copy.wait_recv()
    own_back.wait()
    for copy in started:
        copy.wait_send()
    for copy, here in conditional:

        @pl.when(jnp.logical_not(here))
        def _(copy=copy):
            copy.wait_send()


def shards(queries, keys, values, prefix_keys, prefix_values, grad_out, lengths):
    vmem = pl.BlockSpec(memory_space=pltpu.VMEM)
    anywhere = pl.BlockSpec(memory_space=pl.ANY)
    smem = pl.BlockSpec(memory_space=pltpu.SMEM)

    def sems(*dims):
        return pltpu.SemaphoreType.DMA((2, *dims))

    grads = pl.pallas_call(
        kernel,
        out_shape=(
            jax.ShapeDtypeStruct((HALF, NC * NY * LANES), BF16),
            jax.ShapeDtypeStruct((HALF, 4 * HD), BF16),
            jax.ShapeDtypeStruct((HALF, 4 * HD), BF16),
            jax.ShapeDtypeStruct((2, 2 * HD), BF16),
            jax.ShapeDtypeStruct((2, 2 * HD), BF16),
        ),
        in_specs=[smem, anywhere, anywhere, anywhere, anywhere, vmem, vmem],
        out_specs=(anywhere, vmem, vmem, vmem, vmem),
        scratch_shapes=[
            pltpu.VMEM((NY, BLOCK, LANES), BF16),
            pltpu.VMEM((NY, BLOCK, LANES), BF16),
            pltpu.VMEM((NZH, 2, 2, BLOCK, HD), BF16),
            pltpu.VMEM((NZH, 2, NY, BLOCK, HD), BF16),
            pltpu.VMEM((NZ * 8, HD), F32),
            pltpu.VMEM((4, NX * 32, HD), BF16),
            pltpu.VMEM((2, PROMPT, HD), BF16),
            pltpu.VMEM((NY, PROMPT, LANES), BF16),
            pltpu.VMEM((NY, PROMPT, LANES), BF16),
            pltpu.VMEM((NY, PROMPT, LANES), BF16),
            pltpu.VMEM((NZH, SEEN, LANES), BF16),
            pltpu.VMEM((NZH, SEEN, LANES), BF16),
            pltpu.VMEM((NZH, SEEN, LANES), BF16),
            pltpu.VMEM((NY, 8, LANES), F32),
            pltpu.VMEM((NY, 8, LANES), F32),
            pltpu.VMEM((NY, HD, LANES), F32),
            pltpu.VMEM((5, 2, NY * BLOCK, HD), F32),
            pltpu.VMEM((5, NY * BLOCK, HD), F32),
            pltpu.VMEM((NZH, NY * BLOCK, HD), BF16),
            pltpu.VMEM((NZH, 2, NY, HALF, HD), BF16),
            pltpu.VMEM((2, NY, HALF, HD), BF16),
            pltpu.VMEM((6, NY, HALF, HD), BF16),
            pltpu.VMEM((PROMPT, HD), F32),
            pltpu.VMEM((4, NX * 32, HD), F32),
            pltpu.VMEM((NX - 1, 4, 32, HD), F32),
            pltpu.VMEM((NZ * 8, HD), F32),
            pltpu.VMEM((NZ - 1, 8, HD), F32),
            pltpu.VMEM((NY, BLOCK, LANES), BF16),
            sems(NZ - 1),
            sems(6),
            pltpu.SemaphoreType.DMA((4,)),
            pltpu.SemaphoreType.DMA((NY,)),
            sems(NY * NC - 1),
            pltpu.SemaphoreType.DMA((NZH, 4)),
            pltpu.SemaphoreType.DMA((NZH, NY)),
            sems(5),
            sems(NX - 1),
            pltpu.SemaphoreType.DMA((4,)),
            pltpu.SemaphoreType.DMA((NY,)),
            sems(5),
            sems(NZH, NY * NC - 1),
            sems(6),
            pltpu.SemaphoreType.DMA((NY,)),
            pltpu.SemaphoreType.DMA((4,)),
            sems(NX - 1),
            sems(NZ - 1),
            sems(NY * NC - 1),
            pltpu.SemaphoreType.DMA((13,)),
        ],
        compiler_params=pltpu.CompilerParams(
            collective_id=0, has_side_effects=True, vmem_limit_bytes=VMEM_BYTES
        ),
        name="attention_grads",
    )(lengths, queries[0], keys[0], values[0], grad_out[0], prefix_keys, prefix_values)

    return (grads[0][None], grads[1][None], grads[2][None], grads[3], grads[4])


def solution(mesh):
    in_specs = (
        P("resp", "pre", "head"),
        P("resp", "pre", "head"),
        P("resp", "pre", "head"),
        P(("resp", "pre"), "head"),
        P(("resp", "pre"), "head"),
        P("resp", ("pre", "head"), None),
        P("resp"),
    )
    out_specs = (
        P("resp", ("pre", "head"), None),
        P("resp", ("pre", "head"), None),
        P("resp", ("pre", "head"), None),
        P(("resp", "pre"), "head"),
        P(("resp", "pre"), "head"),
    )
    return jax.shard_map(shards, mesh=mesh, in_specs=in_specs, out_specs=out_specs, check_vma=False)
```

```python
import functools
import math

import jax
import jax.numpy as jnp
from jax import lax
from jax.experimental import pallas as pl
from jax.experimental.pallas import tpu as pltpu
from jax.sharding import PartitionSpec as P

HD = 128
SOFTCAP = 50.0
SCORE_FACTOR = 1.0 / (math.sqrt(HD) * SOFTCAP)
EXP2_FACTOR = SOFTCAP * math.log2(math.e)
INV_ROOT = 1.0 / math.sqrt(HD)

NX, NZL, NY, NZH, NC = 4, 4, 4, 4, 2
NZ = NZL * NZH
BLOCK = 128
HALF = BLOCK // NC
LANES = 512
PROMPT = 512
VMEM_BYTES = 62 * 2**20
BASE = [BLOCK * (yb * (yb + 1) // 2) for yb in range(NY)]
SEEN = BLOCK * (NY * (NY + 1) // 2)
OWN, LEFT, RIGHT, FAR = range(4)
MESH = pl.DeviceIdType.MESH

F32 = jnp.float32
BF16 = jnp.bfloat16


def dot(a, b):
    return jnp.dot(a, b, preferred_element_type=F32)


def dot_rows(a, b):
    return lax.dot_general(a, b, (((1,), (1,)), ((), ())), preferred_element_type=F32)


def dot_first(a, b):
    return lax.dot_general(a, b, (((0,), (0,)), ((), ())), preferred_element_type=F32)


def stack_heads(rows):
    return jnp.concatenate([rows[:, h * HD : (h + 1) * HD] for h in range(4)], axis=0)


def kernel(
    len_ref, q_ref, k_ref, v_ref, g_ref, pk_ref, pv_ref,
    gq_ref, gk_ref, gv_ref, gpk_ref, gpv_ref,
    qb, gb, kvz, kva, pz, px, pkv,
    ep, wp, dp, er, wr, dr,
    tot, rdot, dqt, acc, other, send_kv, recv_kv, send_z, recv_z,
    send_p, part_p, recv_x, tile_p, recv_t, out_q,
    sem_pz, sem_z, sem_qs, sem_qr, sem_g, sem_kvs, sem_kvr, sem_ex, sem_px, sem_pys, sem_pyr,
    sem_rx, sem_rs, sem_zr, sem_sps, sem_spr, sem_sx, sem_st, sem_oq, sem_own,
):
    resp, pre, core = (lax.axis_index(a) for a in ("resp", "pre", "head"))
    x, zl = resp // NZL, resp % NZL
    y, zh = pre // NZH, pre % NZH
    z = zh * NZL + zl
    left, right, far = (zh + NZH - 1) % NZH, (zh + 1) % NZH, (zh + 2) % NZH
    place_of = [zh, left, right, far]

    def device(x=x, zl=zl, y=y, zh=zh, core=core):
        return {"resp": x * NZL + zl, "pre": y * NZH + zh, "head": core}

    z_partners = [
        ((zl + a) % NZL, (zh + b) % NZH) for b in range(NZH) for a in range(NZL) if a or b
    ]
    yc_partners = [
        ((y + a) % NY, (core + b) % NC) for a in range(NY) for b in range(NC) if a or b
    ]
    x_partners = [(x + a) % NX for a in range(1, NX)]

    started = []

    def send(src, dst, sems, index, to):
        copy = pltpu.make_async_remote_copy(
            src_ref=src,
            dst_ref=dst,
            send_sem=sems.at[(0, *index)],
            recv_sem=sems.at[(1, *index)],
            device_id=to,
            device_id_type=MESH,
        )
        copy.start()
        started.append(copy)
        return copy

    conditional = []

    def deliver(src, dst, send_sem, recv_sem, to, here):
        copy = pltpu.make_async_remote_copy(
            src_ref=src,
            dst_ref=dst,
            send_sem=send_sem,
            recv_sem=recv_sem,
            device_id=to,
            device_id_type=MESH,
        )

        @pl.when(here)
        def _():
            pltpu.make_async_copy(src, dst, recv_sem).start()

        @pl.when(jnp.logical_not(here))
        def _():
            copy.start()

        conditional.append((copy, here))

    def delivered(dst, recv_sem):
        pltpu.make_async_copy(dst, dst, recv_sem).wait()

    def local(src, dst, index):
        copy = pltpu.make_async_copy(src, dst, sem_own.at[index])
        copy.start()
        return copy

    def cols(start, width):
        return pl.ds(pl.multiple_of(start, HD), width)

    def rows(start, count):
        return pl.ds(pl.multiple_of(start, 16), count)

    packed = [
        local(ref.at[:, pl.ds(g * HD, HD)], kvz.at[zh, g, which], 2 + 2 * g + which)
        for g in range(2)
        for which, ref in enumerate((k_ref, v_ref))
    ]
    mine_g = cols(y * (NC * LANES) + core * LANES, LANES)
    own_grads = local(g_ref.at[:, mine_g], gb.at[y, rows(core * HALF, HALF)], 1)
    mine_z = pl.ds(pl.multiple_of(z * 8, 8), 8)
    pz[mine_z, :] = jnp.concatenate(
        [
            ref[:, g * HD : (g + 1) * HD].astype(F32)
            for ref in (pk_ref, pv_ref)
            for g in range(2)
        ],
        axis=0,
    )

    barrier = pltpu.get_barrier_semaphore()
    greeted = [device(zl=a, zh=b) for a, b in z_partners]
    greeted += [device(y=a, core=b) for a, b in yc_partners]
    greeted += [device(x=a) for a in x_partners]
    for to in greeted:
        pl.semaphore_signal(barrier, inc=1, device_id=to, device_id_type=MESH)
    pl.semaphore_wait(barrier, len(greeted))

    pieces = [
        send(pz.at[mine_z], pz.at[mine_z], sem_pz, (i,), device(zl=a, zh=b))
        for i, (a, b) in enumerate(z_partners)
    ]

    for copy in packed:
        copy.wait()
    left_first = send(kvz.at[zh, 0], kvz.at[zh, 0], sem_z, (0,), device(zh=right))
    right_first = send(kvz.at[zh, 1], kvz.at[zh, 1], sem_z, (1,), device(zh=left))

    takers = [
        (j, b, 2 * core + j, jnp.logical_and(y == 2 * core + j, core == b))
        for j in range(2)
        for b in range(NC)
    ]

    def spread(step):
        zs = place_of[step]
        for i, (j, b, a, here) in enumerate(takers):
            deliver(
                kvz.at[zs, j] if step == FAR else kvz.at[zs, j, b],
                kva.at[zs, :, y] if step == FAR else kva.at[zs, b, y],
                sem_kvs.at[step, i], sem_kvr.at[step, y], device(y=a, core=b), here,
            )

    def swap(step):
        zs = place_of[step]
        for a in range(NY):
            delivered(kva.at[zs, core, a], sem_kvr.at[step, a])
        return send(kva.at[zs, core], kva.at[zs, core], sem_ex, (step,), device(core=1 - core))

    for i, (j, b, a, here) in enumerate(takers):
        deliver(
            q_ref.at[:, pl.ds((j * NC + b) * LANES, LANES)], qb.at[y],
            sem_qs.at[i], sem_qr.at[y], device(y=a, core=b), here,
        )
    spread(OWN)
    grads_in = [
        send(
            g_ref.at[:, cols(a * (NC * LANES) + b * LANES, LANES)],
            gb.at[y, rows(core * HALF, HALF)],
            sem_g,
            (i,),
            device(y=a, core=b),
        )
        for i, (a, b) in enumerate(yc_partners)
    ]
    left_second = send(kvz.at[zh, 1], kvz.at[zh, 1], sem_z, (2,), device(zh=right))
    right_second = send(kvz.at[zh, 0], kvz.at[zh, 0], sem_z, (3,), device(zh=left))

    for copy in pieces:
        copy.wait_recv()
    mine_x = pl.ds(pl.multiple_of(x * 32, 32), 32)
    for t in range(4):
        for k in range(2):
            piece = pz[pl.ds(t * 2 + k, NZ, stride=8), :].astype(BF16)
            px[t, pl.ds(pl.multiple_of(x * 32 + k * 16, 16), 16), :] = piece
    prompt_x = [
        send(px.at[:, mine_x], px.at[:, mine_x], sem_px, (i,), device(x=a))
        for i, a in enumerate(x_partners)
    ]

    left_first.wait_recv()
    far_0 = send(kvz.at[left, 0], kvz.at[left, 0], sem_z, (4,), device(zh=right))
    right_first.wait_recv()
    far_1 = send(kvz.at[right, 1], kvz.at[right, 1], sem_z, (5,), device(zh=left))

    swapped = [swap(OWN), None, None, None]
    for copy in prompt_x:
        copy.wait_recv()
    mine_y = pl.ds(pl.multiple_of(y * BLOCK, BLOCK), BLOCK)
    for i, (j, b, a, here) in enumerate(takers):
        deliver(
            px.at[2 * b + j], pkv.at[b, mine_y],
            sem_pys.at[i], sem_pyr.at[y], device(y=a, core=b), here,
        )

    left_second.wait_recv()
    spread(LEFT)
    right_second.wait_recv()
    spread(RIGHT)

    for a in range(NY):
        delivered(qb.at[a], sem_qr.at[a])
    for copy in grads_in:
        copy.wait_recv()
    own_grads.wait()
    length = len_ref[0]
    for yb in range(NY):
        pos = lax.broadcasted_iota(jnp.int32, (BLOCK, LANES), 0) + (yb * NZH + zh) * BLOCK
        gb[yb] = jnp.where(pos < length, gb[yb].astype(F32), 0.0).astype(BF16)
        tot[yb] = jnp.zeros((8, LANES), F32)
        rdot[yb] = jnp.zeros((8, LANES), F32)
        dqt[yb] = jnp.zeros((HD, LANES), F32)

    key_at = lax.broadcasted_iota(jnp.int32, (BLOCK, LANES), 0)
    query_at = lax.broadcasted_iota(jnp.int32, (BLOCK, LANES), 1) % BLOCK
    gap = key_at - query_at

    def response_keys(step):
        return lambda c: kva[place_of[step], 0, c]

    def response_values(step):
        return lambda c: kva[place_of[step], 1, c]

    def prompt_keys(c):
        return pkv[0, pl.ds(c * BLOCK, BLOCK), :]

    def prompt_values(c):
        return pkv[1, pl.ds(c * BLOCK, BLOCK), :]

    def first_pass(yb, keys, values, count, e_ref, w_ref, d_ref, base, limit):
        queries, grads = stack_heads(qb[yb]), stack_heads(gb[yb])
        total, row_dot = tot[yb], rdot[yb]
        for c in range(count):
            score = dot_rows(keys(c), queries)
            grad_prob = dot_rows(values(c), grads)
            tangent = jnp.tanh(score * SCORE_FACTOR)
            weight = jnp.exp2(tangent * EXP2_FACTOR)
            if limit is not None and c == count - 1:
                weight = jnp.where(gap <= limit, weight, 0.0)
            slope = weight * (1.0 - tangent * tangent)
            total = total + weight.reshape(BLOCK // 8, 8, LANES).sum(0)
            row_dot = row_dot + (weight * grad_prob).reshape(BLOCK // 8, 8, LANES).sum(0)
            to = pl.ds(base + c * BLOCK, BLOCK)
            e_ref[to, :] = weight.astype(BF16)
            w_ref[to, :] = slope.astype(BF16)
            d_ref[to, :] = grad_prob.astype(BF16)
        tot[yb] = total
        rdot[yb] = row_dot

    def response_first(step):
        zs = place_of[step]
        limit = (zh - zs) * BLOCK
        if step == FAR:
            for a in range(NY):
                delivered(kva.at[zs, :, a], sem_kvr.at[step, a])
        else:
            swapped[step].wait_recv()
        for yb in range(NY):
            first_pass(
                yb, response_keys(step), response_values(step), yb + 1,
                er.at[step], wr.at[step], dr.at[step], BASE[yb], limit,
            )

    response_first(OWN)
    for a in range(NY):
        delivered(pkv.at[core, pl.ds(a * BLOCK, BLOCK)], sem_pyr.at[a])
    swapped_prompt = send(pkv.at[core], pkv.at[core], sem_ex, (4,), device(core=1 - core))
    swapped[LEFT] = swap(LEFT)
    swapped[RIGHT] = swap(RIGHT)

    swapped_prompt.wait_recv()
    for yb in range(NY):
        first_pass(
            yb, prompt_keys, prompt_values, PROMPT // BLOCK,
            ep.at[yb], wp.at[yb], dp.at[yb], 0, None,
        )

    far_0.wait_recv()
    far_1.wait_recv()
    spread(FAR)
    response_first(LEFT)
    response_first(RIGHT)
    response_first(FAR)

    for yb in range(NY):
        total = jnp.sum(tot[yb], axis=0, keepdims=True)
        row_dot = jnp.sum(rdot[yb], axis=0, keepdims=True)
        inverse = 1.0 / total
        tot[yb] = jnp.broadcast_to(inverse, (8, LANES))
        rdot[yb] = jnp.broadcast_to(row_dot * inverse, (8, LANES))

    def second_pass(yb, keys, count, e_ref, w_ref, d_ref, base, fresh, acc):
        queries, grads = stack_heads(qb[yb]), stack_heads(gb[yb])
        inverse = tot[yb, 0:1, :]
        inverse_root = inverse * INV_ROOT
        row_dot = rdot[yb, 0:1, :]
        query_grad = dqt[yb]
        for c in range(count):
            at = pl.ds(base + c * BLOCK, BLOCK)
            to = pl.ds(c * BLOCK, BLOCK)
            prob = (e_ref[at, :].astype(F32) * inverse).astype(BF16)
            grad_score = (
                (w_ref[at, :].astype(F32) * inverse_root) * (d_ref[at, :].astype(F32) - row_dot)
            ).astype(BF16)
            key_grad = dot(grad_score, queries)
            value_grad = dot(prob, grads)
            query_grad = query_grad + dot_first(keys(c), grad_score)
            if fresh(c):
                acc[0, to, :] = key_grad
                acc[1, to, :] = value_grad
            else:
                acc[0, to, :] += key_grad
                acc[1, to, :] += value_grad
        dqt[yb] = query_grad

    def trade(step):
        return send(acc.at[step, 1 - core], other.at[step], sem_rx, (step,), device(core=1 - core))

    partials = [None] * 4
    traded = [None] * 5

    def response_second(step):
        for yb in range(NY):
            second_pass(
                yb, response_keys(step), yb + 1,
                er.at[step], wr.at[step], dr.at[step], BASE[yb], lambda c, yb=yb: c == yb,
                acc.at[step],
            )
        traded[step] = trade(step)

    def hand_out(step):
        traded[step].wait_recv()
        send_kv[step] = (acc[step, core] + other[step]).astype(BF16)
        partials[step] = [
            send(
                send_kv.at[step, rows(a * BLOCK + b * HALF, HALF)],
                recv_kv.at[step, core, y],
                sem_rs,
                (step, i),
                device(y=a, core=b),
            )
            for i, (a, b) in enumerate(yc_partners)
        ]
        recv_kv[step, core, y] = send_kv[step, rows(y * BLOCK + core * HALF, HALF), :]

    def collect(step):
        for copy in partials[step]:
            copy.wait_recv()

    response_second(FAR)

    for yb in range(NY):
        second_pass(
            yb, prompt_keys, PROMPT // BLOCK, ep.at[yb], wp.at[yb], dp.at[yb], 0,
            lambda c, yb=yb: yb == 0, acc.at[4],
        )
    traded[4] = trade(4)
    hand_out(FAR)
    response_second(LEFT)

    traded[4].wait_recv()
    send_p[...] = acc[4, core] + other[4]
    for a in range(NY):
        deliver(
            send_p.at[pl.ds(a * BLOCK, BLOCK)], part_p.at[2 * core + y % 2],
            sem_sps.at[a], sem_spr.at[2 * core + y % 2], device(y=a, core=y // 2),
            jnp.logical_and(y == a, core == y // 2),
        )
    collect(FAR)
    far_key = send(recv_kv.at[FAR, 0], recv_z.at[0], sem_zr, (0,), device(zh=right))
    far_value = send(recv_kv.at[FAR, 1], recv_z.at[1], sem_zr, (1,), device(zh=left))
    hand_out(LEFT)
    response_second(RIGHT)

    for t in range(4):
        delivered(part_p.at[t], sem_spr.at[t])
    prompt_x_back = [
        send(
            part_p.at[:, pl.ds(pl.multiple_of(a * 32, 32), 32)],
            recv_x.at[i],
            sem_sx,
            (i,),
            device(x=a),
        )
        for i, a in enumerate(x_partners)
    ]
    collect(LEFT)
    key_right = send(recv_kv.at[LEFT, 0], recv_z.at[4], sem_zr, (4,), device(zh=left))
    hand_out(RIGHT)
    response_second(OWN)

    for yb in range(NY):
        for h in range(4):
            at = pl.ds(h * HD, HD)
            out_q[yb, :, at] = dqt[yb, :, at].T.astype(BF16)
    query_back = [
        send(
            out_q.at[a, rows(b * HALF, HALF)],
            gq_ref.at[:, mine_g],
            sem_oq,
            (i,),
            device(y=a, core=b),
        )
        for i, (a, b) in enumerate(yc_partners)
    ]
    own_back = local(out_q.at[y, rows(core * HALF, HALF)], gq_ref.at[:, mine_g], 12)

    for copy in prompt_x_back:
        copy.wait_recv()
    for t in range(4):
        part = part_p[t, mine_x, :]
        for i in range(NX - 1):
            part = part + recv_x[i, t]
        for k in range(2):
            tile_p[pl.ds(t * 2 + k, NZ, stride=8), :] = part[k * 16 : (k + 1) * 16]
    tiles_back = [
        send(
            tile_p.at[pl.ds(pl.multiple_of((b * NZL + a) * 8, 8), 8)],
            recv_t.at[i],
            sem_st,
            (i,),
            device(zl=a, zh=b),
        )
        for i, (a, b) in enumerate(z_partners)
    ]

    collect(RIGHT)
    value_left = send(recv_kv.at[RIGHT, 1], recv_z.at[3], sem_zr, (3,), device(zh=right))
    hand_out(OWN)
    far_key.wait_recv()
    send_z[0] = (recv_kv[RIGHT, 0].astype(F32) + recv_z[0].astype(F32)).astype(BF16)
    key_left = send(send_z.at[0], recv_z.at[2], sem_zr, (2,), device(zh=right))
    far_value.wait_recv()
    send_z[1] = (recv_kv[LEFT, 1].astype(F32) + recv_z[1].astype(F32)).astype(BF16)
    value_right = send(send_z.at[1], recv_z.at[5], sem_zr, (5,), device(zh=left))

    collect(OWN)
    key_left.wait_recv()
    key_right.wait_recv()
    value_left.wait_recv()
    value_right.wait_recv()
    for which, ref, first, second in ((0, gk_ref, 2, 4), (1, gv_ref, 3, 5)):
        for a in range(NY):
            total = recv_kv[OWN, which, a].astype(F32) + recv_z[first, a].astype(F32)
            ref[:, pl.ds(a * HD, HD)] = (total + recv_z[second, a].astype(F32)).astype(BF16)

    for copy in tiles_back:
        copy.wait_recv()
    tile = tile_p[mine_z, :]
    for i in range(NZ - 1):
        tile = tile + recv_t[i]
    for which, ref in enumerate((gpk_ref, gpv_ref)):
        for g in range(2):
            at = 4 * which + 2 * g
            ref[:, pl.ds(g * HD, HD)] = tile[at : at + 2].astype(BF16)

    for copy in query_back:
        copy.wait_recv()
    own_back.wait()
    for copy in started:
        copy.wait_send()
    for copy, here in conditional:

        @pl.when(jnp.logical_not(here))
        def _(copy=copy):
            copy.wait_send()


def shards(queries, keys, values, prefix_keys, prefix_values, grad_out, lengths):
    vmem = pl.BlockSpec(memory_space=pltpu.VMEM)
    anywhere = pl.BlockSpec(memory_space=pl.ANY)
    smem = pl.BlockSpec(memory_space=pltpu.SMEM)

    def sems(*dims):
        return pltpu.SemaphoreType.DMA((2, *dims))

    grads = pl.pallas_call(
        kernel,
        out_shape=(
            jax.ShapeDtypeStruct((HALF, NC * NY * LANES), BF16),
            jax.ShapeDtypeStruct((HALF, 4 * HD), BF16),
            jax.ShapeDtypeStruct((HALF, 4 * HD), BF16),
            jax.ShapeDtypeStruct((2, 2 * HD), BF16),
            jax.ShapeDtypeStruct((2, 2 * HD), BF16),
        ),
        in_specs=[smem, anywhere, anywhere, anywhere, anywhere, vmem, vmem],
        out_specs=(anywhere, vmem, vmem, vmem, vmem),
        scratch_shapes=[
            pltpu.VMEM((NY, BLOCK, LANES), BF16),
            pltpu.VMEM((NY, BLOCK, LANES), BF16),
            pltpu.VMEM((NZH, 2, 2, BLOCK, HD), BF16),
            pltpu.VMEM((NZH, 2, NY, BLOCK, HD), BF16),
            pltpu.VMEM((NZ * 8, HD), F32),
            pltpu.VMEM((4, NX * 32, HD), BF16),
            pltpu.VMEM((2, PROMPT, HD), BF16),
            pltpu.VMEM((NY, PROMPT, LANES), BF16),
            pltpu.VMEM((NY, PROMPT, LANES), BF16),
            pltpu.VMEM((NY, PROMPT, LANES), BF16),
            pltpu.VMEM((NZH, SEEN, LANES), BF16),
            pltpu.VMEM((NZH, SEEN, LANES), BF16),
            pltpu.VMEM((NZH, SEEN, LANES), BF16),
            pltpu.VMEM((NY, 8, LANES), F32),
            pltpu.VMEM((NY, 8, LANES), F32),
            pltpu.VMEM((NY, HD, LANES), F32),
            pltpu.VMEM((5, 2, NY * BLOCK, HD), F32),
            pltpu.VMEM((5, NY * BLOCK, HD), F32),
            pltpu.VMEM((NZH, NY * BLOCK, HD), BF16),
            pltpu.VMEM((NZH, 2, NY, HALF, HD), BF16),
            pltpu.VMEM((2, NY, HALF, HD), BF16),
            pltpu.VMEM((6, NY, HALF, HD), BF16),
            pltpu.VMEM((PROMPT, HD), F32),
            pltpu.VMEM((4, NX * 32, HD), F32),
            pltpu.VMEM((NX - 1, 4, 32, HD), F32),
            pltpu.VMEM((NZ * 8, HD), F32),
            pltpu.VMEM((NZ - 1, 8, HD), F32),
            pltpu.VMEM((NY, BLOCK, LANES), BF16),
            sems(NZ - 1),
            sems(6),
            pltpu.SemaphoreType.DMA((4,)),
            pltpu.SemaphoreType.DMA((NY,)),
            sems(NY * NC - 1),
            pltpu.SemaphoreType.DMA((NZH, 4)),
            pltpu.SemaphoreType.DMA((NZH, NY)),
            sems(5),
            sems(NX - 1),
            pltpu.SemaphoreType.DMA((4,)),
            pltpu.SemaphoreType.DMA((NY,)),
            sems(5),
            sems(NZH, NY * NC - 1),
            sems(6),
            pltpu.SemaphoreType.DMA((NY,)),
            pltpu.SemaphoreType.DMA((4,)),
            sems(NX - 1),
            sems(NZ - 1),
            sems(NY * NC - 1),
            pltpu.SemaphoreType.DMA((13,)),
        ],
        compiler_params=pltpu.CompilerParams(
            collective_id=0, has_side_effects=True, vmem_limit_bytes=VMEM_BYTES
        ),
        name="attention_grads",
    )(lengths, queries[0], keys[0], values[0], grad_out[0], prefix_keys, prefix_values)

    return (grads[0][None], grads[1][None], grads[2][None], grads[3], grads[4])


def solution(mesh):
    in_specs = (
        P("resp", "pre", "head"),
        P("resp", "pre", "head"),
        P("resp", "pre", "head"),
        P(("resp", "pre"), "head"),
        P(("resp", "pre"), "head"),
        P("resp", ("pre", "head"), None),
        P("resp"),
    )
    out_specs = (
        P("resp", ("pre", "head"), None),
        P("resp", ("pre", "head"), None),
        P("resp", ("pre", "head"), None),
        P(("resp", "pre"), "head"),
        P(("resp", "pre"), "head"),
    )
    return jax.shard_map(shards, mesh=mesh, in_specs=in_specs, out_specs=out_specs, check_vma=False)
```
